32 devices in a mesh: groups: 2 (over y), fsdp: 4 (over z), tenant: 2 (over x), pair: 2 (over core).
Axes of the slice: x: 2, y: 2, z: 4, core: 2. Of those that a mesh axis runs over, the one named last changes fastest.
Arguments:
- hidden: bfloat16 [2, 32, 128, 8192], P('pair', ('groups', 'fsdp', 'tenant')), parts along dimension 1, may hold values from -6 to 6
- pair_adapter_index: int32 [32], P(('groups', 'fsdp', 'tenant')), parts along dimension 0, may hold values from 0 to 3
- live_block_count: int32 [16], P(('groups', 'fsdp', 'tenant')), parts along dimension 0, may hold values from 0 to 2, as said below
- lengths: int32 [2, 32], P('pair', ('groups', 'fsdp', 'tenant')), parts along dimension 1, may hold values from 1 to 128, as said below
- adapter_storage_row: int32 [4], replicated, may hold values from 0 to 3, each once
- frozen_base_weight: bfloat16 [8192, 512], P(('fsdp', 'pair')), may hold values from -0.0625 to 0.0625
- adapter_down_maps: bfloat16 [4, 8192, 64], P('tenant', ('fsdp', 'pair')), may hold values from -0.0625 to 0.0625
- adapter_up_maps: bfloat16 [4, 512, 64], P('tenant', ('fsdp', 'pair')), may hold values from -0.75 to 0.75
- readout: float32 [512], replicated, may hold values from -6 to 6
- reference_score_margin: float32 [32], P(('groups', 'fsdp', 'tenant')), parts along dimension 0, may hold values from -600 to 600
Outputs:
- pair_loss: float32 [32], P(('groups', 'fsdp', 'tenant')), parts along dimension 0
- down_gradient: bfloat16 [8, 8192, 64], P(('groups', 'tenant'), ('fsdp', 'pair')), parts along dimension 0
- up_gradient: bfloat16 [8, 512, 64], P(('groups', 'tenant'), ('fsdp', 'pair')), parts along dimension 0
The draws below stay inside these ranges and needn't reach their ends.
There are 2 independent parts, one for each index of `groups`. The reference program is written for one: setup_inputs(seed, part) draws one part's arguments, and reference() takes and returns one part's arrays. A program takes and returns all parts, laid end to end along the dimension named above; an argument that names none is the same for every part. Nothing has to cross between parts.
Inputs may be any that keep to these rules, and one draw needn't show every extreme that they name: A holder's first live_block_count slots hold live pairs, the rest are padding. A block's first lengths positions are live. `adapter_storage_row`: each storage row once.
All inputs are finite; a program needn't handle non-finite values.
Results may differ from the reference program's by a relative error of at most 0.0068.
Values may be sent and summed in bfloat16 or wider, within the bound.
A program may use at most 64 MiB of HBM per device.

```python
import math
import jax
import jax.numpy as jnp
import numpy as np
from jax import lax

MODEL_WIDTH = 8192
OUTPUT_WIDTH = 512
ADAPTER_RANK = 64
BLOCK = 128
BLK_CAP = 2
ADAPTER_TOTAL = 4
HOLDERS = 8
SLOTS = 16


def draw_live_block_count(key, part):
    key = jax.random.fold_in(key, 11)
    first_key, second_key = jax.random.split(key)
    counts = jax.random.randint(first_key, (HOLDERS,), 0, BLK_CAP + 1)
    target = jax.random.randint(second_key, (), 0, HOLDERS)
    return counts.at[target].set(BLK_CAP).astype(jnp.int32)


def draw_lengths(key, part):
    key = jax.random.fold_in(key, 23)
    first_key, second_key = jax.random.split(key)
    values = jax.random.randint(first_key, (2, SLOTS), 1, BLOCK + 1)
    target = jax.random.randint(second_key, (2,), 0, SLOTS)
    values = values.at[0, target[0]].set(BLOCK)
    values = values.at[1, target[1]].set(BLOCK)
    return values.astype(jnp.int32)


def place_ends(values, rng, least, high):
    longest = values.shape.index(max(values.shape))
    spots = []
    for shift in (0, 1):
        where = [jax.random.randint(jax.random.fold_in(rng, axis), (), 0, length) for axis, length in enumerate(values.shape)]
        where[longest] = (where[longest] + shift) % values.shape[longest]
        spots.append(tuple(where))
    return values.at[spots[0]].set(least).at[spots[1]].set(high)


def shard_levels(stream_key, dims, cuts, least, top_value):
    level, own = 1.0, jax.random.fold_in(stream_key, 6)
    for dim, shards_of in cuts:
        heights = jnp.exp(jax.random.uniform(jax.random.fold_in(own, dim), (shards_of,), jnp.float32, least / len(cuts), top_value / len(cuts)))
        level = level * jnp.repeat(heights, dims[dim] // shards_of).reshape([-1 if axis == dim else 1 for axis in range(len(dims))])
    return level


def cumulative_ranks(amount, skew):
    loads = [(1 << 20) // math.isqrt(standing ** skew) + 1 for standing in range(1, amount + 1)]
    deviation = 1 + sum(loads) // (1 << 30)
    return np.cumsum(np.array([max(1, weight // deviation) for weight in loads]))


def ranked(stream_key, shape, count, lean):
    listing = cumulative_ranks(count, lean)
    ticket = jax.random.randint(jax.random.fold_in(stream_key, 1), shape, 0, int(listing[count - 1]))
    grade = jnp.searchsorted(jnp.asarray(listing, jnp.int32), ticket, side="right")
    return jax.random.permutation(jax.random.fold_in(stream_key, 2), count)[grade].astype(jnp.int32)


def normal_values(key, shape, width, bound, shards=(), kind=jnp.bfloat16):
    values = width * jax.random.normal(key, shape, jnp.float32)
    if shards:
        values = values * shard_levels(key, shape, shards, -0.22, 0.18)
    return jnp.clip(values, -bound, bound).astype(kind)


def setup_inputs(seed: int = 0, part: int = 0) -> dict:
    streams_of = jax.random.split(jax.random.key(seed), 11)
    own_keys = jax.random.split(jax.random.fold_in(streams_of[10], part), 11)
    hidden = normal_values(own_keys[0], (2, SLOTS, BLOCK, MODEL_WIDTH), 1.0, 6.0, ((0, 2), (1, 8)))
    pair_adapter_index = place_ends(ranked(own_keys[1], (SLOTS,), ADAPTER_TOTAL, 2), jax.random.fold_in(own_keys[1], 3), 0, ADAPTER_TOTAL - 1).astype(jnp.int32)
    live_block_count = draw_live_block_count(jax.random.fold_in(jax.random.fold_in(streams_of[10], part), 71), part)
    lengths = draw_lengths(jax.random.fold_in(jax.random.fold_in(streams_of[10], part), 71), part)
    adapter_storage_row = jax.random.permutation(streams_of[4], ADAPTER_TOTAL).astype(jnp.int32)
    frozen_base_weight = normal_values(streams_of[5], (MODEL_WIDTH, OUTPUT_WIDTH), MODEL_WIDTH ** -0.5, 0.0625, ((0, 8),))
    adapter_down_maps = normal_values(streams_of[6], (ADAPTER_TOTAL, MODEL_WIDTH, ADAPTER_RANK), MODEL_WIDTH ** -0.5, 0.0625, ((0, 2), (1, 8)))
    adapter_up_maps = normal_values(streams_of[7], (ADAPTER_TOTAL, OUTPUT_WIDTH, ADAPTER_RANK), ADAPTER_RANK ** -0.5, 0.75, ((0, 2), (1, 8)))
    readout = normal_values(streams_of[8], (OUTPUT_WIDTH,), 1.0, 6.0, (), jnp.float32)
    reference_score_margin = normal_values(own_keys[9], (SLOTS,), 100.0, 600.0, ((0, 8),), jnp.float32)
    return {"hidden": hidden, "pair_adapter_index": pair_adapter_index, "live_block_count": live_block_count, "lengths": lengths, "adapter_storage_row": adapter_storage_row, "frozen_base_weight": frozen_base_weight, "adapter_down_maps": adapter_down_maps, "adapter_up_maps": adapter_up_maps, "readout": readout, "reference_score_margin": reference_score_margin}


beta_value = 0.01


def reference(hidden, pair_adapter_index, live_block_count, lengths, adapter_storage_row, frozen_base_weight, adapter_down_maps, adapter_up_maps, readout, reference_score_margin):
    adapter_slot = adapter_storage_row[pair_adapter_index].astype(jnp.int32)
    slot_index = jnp.arange(SLOTS, dtype=jnp.int32)
    alive_mask = (slot_index % BLK_CAP < jnp.repeat(live_block_count, BLK_CAP)).astype(jnp.float32)
    position = jnp.arange(BLOCK, dtype=jnp.int32)
    valid_mask = (position[None, None, :] < lengths[:, :, None]).astype(jnp.float32)
    flat_tokens = hidden.reshape(2 * SLOTS * BLOCK, MODEL_WIDTH)
    base_part = jnp.dot(flat_tokens, frozen_base_weight, preferred_element_type=jnp.float32).reshape(2, SLOTS, BLOCK, OUTPUT_WIDTH)
    half_signs = jnp.array([1.0, -1.0], dtype=jnp.float32)

    def one_slot(state_pair, which):
        down_total, up_total = state_pair
        tokens = lax.dynamic_index_in_dim(hidden, which, 1, keepdims=False).astype(jnp.float32)
        storage_row_index = adapter_slot[which]
        down_projection_map = lax.dynamic_index_in_dim(adapter_down_maps, storage_row_index, 0, keepdims=False).astype(jnp.float32)
        up_projection_map = lax.dynamic_index_in_dim(adapter_up_maps, storage_row_index, 0, keepdims=False).astype(jnp.float32)
        low_rank = jnp.einsum('ptd,dr->ptr', tokens, down_projection_map).astype(jnp.bfloat16)
        adapted = jnp.einsum('ptr,or->pto', low_rank.astype(jnp.float32), up_projection_map)
        mixed_out = lax.dynamic_index_in_dim(base_part, which, 1, keepdims=False) + adapted
        gate_value = jax.nn.sigmoid(mixed_out)
        token_score = jnp.einsum('pto,o->pt', mixed_out * gate_value, readout, precision=lax.Precision.HIGHEST)
        slot_valid = lax.dynamic_index_in_dim(valid_mask, which, 1, keepdims=False)
        seq_score = jnp.sum(slot_valid * token_score, axis=1)
        pair_logit = beta_value * (seq_score[0] - seq_score[1] - reference_score_margin[which])
        loss_value = alive_mask[which] * jax.nn.softplus(-pair_logit)
        factor = -beta_value * jax.nn.sigmoid(-pair_logit) * alive_mask[which] * half_signs
        slope = gate_value * (1.0 + mixed_out * (1.0 - gate_value))
        cotangent = (factor[:, None, None] * slot_valid[:, :, None] * readout * slope).astype(jnp.bfloat16)
        up_term = jnp.einsum('pto,ptr->or', cotangent.astype(jnp.float32), low_rank.astype(jnp.float32))
        low_grad = jnp.einsum('pto,or->ptr', cotangent.astype(jnp.float32), up_projection_map).astype(jnp.bfloat16)
        down_term = jnp.einsum('ptd,ptr->dr', tokens, low_grad.astype(jnp.float32))
        down_total = down_total.at[storage_row_index].add(down_term)
        up_total = up_total.at[storage_row_index].add(up_term)
        return (down_total, up_total), loss_value

    start_state = (jnp.zeros((ADAPTER_TOTAL, MODEL_WIDTH, ADAPTER_RANK), jnp.float32), jnp.zeros((ADAPTER_TOTAL, OUTPUT_WIDTH, ADAPTER_RANK), jnp.float32))
    final_state, pair_loss = lax.scan(one_slot, start_state, slot_index)
    return pair_loss, final_state[0].astype(jnp.bfloat16), final_state[1].astype(jnp.bfloat16)
```

```python
import jax
import jax.numpy as jnp
from jax import lax
from jax.experimental import pallas as pl
from jax.experimental.pallas import tpu as pltpu
from jax.sharding import PartitionSpec as P

BETA = 0.01
F32, BF16 = jnp.float32, jnp.bfloat16
NN = (((1,), (0,)), ((), ()))
NT = (((1,), (1,)), ((), ()))


def dot(a, b, dims=NN):
    return lax.dot_general(a, b, dims, preferred_element_type=F32)


def step_kernel(
    sizes,
    scalars, readout, marks, hidden, base, down, up,
    loss_out, down_out, up_out,
    tokens, wbuf, dbuf, ubuf, mbuf, acc, lacc, pacc, placc,
    score, pscore, lowm, cot, lgt, upsum, upeer, uz, ur, ps, pr, xs, xr, xus, xur,
    loc, locw, tok_s, tok_r, zw_s, zw_r, zd_s, zd_r, zu_s, zu_r, zm_s, zm_r,
    xw_s, xw_r, xd_s, xd_r, yw_s, yw_r, cu_s, cu_r, xu_s, xu_r,
    part_s, part_r, score_s, score_r, mid_s, mid_r, p_s, p_r, q_s, q_r, xg_s, xg_r,
):
    groups, fsdp, tenant, shares, rank = sizes
    g, f = lax.axis_index("groups"), lax.axis_index("fsdp")
    t, p = lax.axis_index("tenant"), lax.axis_index("pair")
    slots, block = 2, tokens.shape[2] // 2
    width = tokens.shape[3]
    lanes = slots * rank
    quarter = g * shares + lax.rem(t, shares)
    side_t = t + 1 - 2 * lax.rem(t, 2)

    def remote(src, dst, send, recv, **where):
        return pltpu.make_async_remote_copy(
            src_ref=src, dst_ref=dst, send_sem=send, recv_sem=recv,
            device_id=where, device_id_type=pl.DeviceIdType.MESH,
        )

    barrier = pltpu.get_barrier_semaphore()
    others = [{"pair": 1 - p}]
    others += [{"fsdp": lax.rem(f + i, fsdp)} for i in range(1, fsdp)]
    others += [{"tenant": lax.rem(t + i, tenant)} for i in range(1, tenant)]
    others += [{"groups": lax.rem(g + i, groups)} for i in range(1, groups)]
    for where in others:
        pl.semaphore_signal(barrier, 1, device_id=where, device_id_type=pl.DeviceIdType.MESH)

    def own_tokens(s):
        return pltpu.make_async_copy(hidden.at[s, p], tokens.at[0, s], loc.at[s])

    local = [
        pltpu.make_async_copy(base, wbuf.at[f], locw.at[0]),
        pltpu.make_async_copy(down, dbuf.at[t, f], locw.at[1]),
        pltpu.make_async_copy(up, ubuf.at[t, f, p], locw.at[2]),
    ]
    for copy in local:
        copy.start()
    own_tokens(f).start()
    pl.semaphore_wait(barrier, len(others))

    def to_z(s, way):
        return {"fsdp": f + 1 - 2 * way}

    def z_w(s, way, src):
        return remote(src, wbuf.at[s, quarter], zw_s.at[s, way], zw_r.at[s], **to_z(s, way))

    def z_d(s, way, src):
        return remote(src, dbuf.at[t, s], zd_s.at[s, way], zd_r.at[s], **to_z(s, way))

    def z_u(s, way, src):
        return remote(src, ubuf.at[t, s, p], zu_s.at[s, way], zu_r.at[s], **to_z(s, way))

    def x_w(s):
        return remote(
            wbuf.at[s, quarter], wbuf.at[s, quarter], xw_s.at[s], xw_r.at[s], tenant=side_t
        )

    def x_d(s, i, src):
        return remote(
            src, dbuf.at[t, s], xd_s.at[s, i], xd_r.at[t, s], tenant=lax.rem(t + i, tenant)
        )

    def x_d_in(s, i):
        other = lax.rem(t + i, tenant)
        return remote(
            dbuf.at[other, s], dbuf.at[other, s], xd_s.at[s, i], xd_r.at[other, s], tenant=other
        )

    def y_w(s, i, which):
        row = g * shares + which
        return remote(
            wbuf.at[s, row], wbuf.at[s, row], yw_s.at[s, i, which], yw_r.at[s, row],
            groups=lax.rem(g + i, groups),
        )

    def y_w_in(s, i, which):
        other = lax.rem(g + i, groups)
        row = other * shares + which
        return remote(
            wbuf.at[s, row], wbuf.at[s, row], yw_s.at[s, i, which], yw_r.at[s, row], groups=other
        )

    def core_tokens(s):
        return remote(
            hidden.at[s, 1 - p], tokens.at[1, s], tok_s.at[s], tok_r.at[s], pair=1 - p
        )

    def z_mark(i):
        return remote(
            marks, mbuf.at[f], zm_s.at[i], zm_r.at[f], fsdp=lax.rem(f + i, fsdp)
        )

    def z_mark_in(i):
        other = lax.rem(f + i, fsdp)
        return remote(mbuf.at[other], mbuf.at[other], zm_s.at[i], zm_r.at[other], fsdp=other)

    for way in (0, 1):

        @pl.when((f < fsdp - 1) if way == 0 else (f > 0))
        def _():
            z_w(f, way, base.at[quarter]).start()
            z_d(f, way, down).start()
            z_u(f, way, up).start()

    for i in range(1, tenant):
        x_d(f, i, down).start()
    core_tokens(f).start()

    def rest(i, carry):
        s = lax.rem(f + i, fsdp)
        own_tokens(s).start()
        core_tokens(s).start()
        return carry

    lax.fori_loop(1, fsdp, rest, 0)
    for i in range(1, fsdp):
        z_mark(i).start()
    mbuf[f] = marks[...]
    acc[...] = jnp.zeros_like(acc)
    lacc[...] = jnp.zeros_like(lacc)
    for copy in local:
        copy.wait()

    column = 256

    def multiply(s):
        own_tokens(s).wait()
        core_tokens(s).wait_recv()
        rows = wbuf.shape[1] * wbuf.shape[2]

        def half(h, carry):
            def columns(c, inner):
                at = pl.ds(pl.multiple_of(c * column, column), column)
                weight = wbuf[s, :, :, at].reshape(rows, column)
                acc[h, :, at] += dot(tokens[h, s], weight)
                return inner

            lax.fori_loop(0, wbuf.shape[3] // column, columns, 0)

            def maps(m, inner):
                at = pl.ds(pl.multiple_of(m * lanes, lanes), lanes)
                lacc[h, :, at] += dot(tokens[h, s], dbuf[m, s], NT)
                return inner

            lax.fori_loop(0, tenant, maps, 0)
            return carry

        lax.fori_loop(0, 2, half, 0)

    for i in range(1, tenant):
        x_d_in(f, i).wait_recv()
    multiply(f)

    def place(k, way):
        s = jnp.where(way == 0, f - k, f + k)
        fine = (k >= 1) & (k < fsdp) & (s >= 0) & (s < fsdp)
        onward = fine & jnp.where(way == 0, f < fsdp - 1, f > 0)
        return jnp.clip(s, 0, fsdp - 1), fine, onward

    def relay(k, way):
        s, fine, onward = place(k, way)

        @pl.when(fine)
        def _():
            z_w(s, way, wbuf.at[s, quarter]).wait_recv()

            @pl.when(onward)
            def _():
                z_w(s, way, wbuf.at[s, quarter]).start()

            if shares > 1:
                x_w(s).start()
            for i in range(1, groups):
                y_w(s, i, lax.rem(t, shares)).start()
            z_d(s, way, dbuf.at[t, s]).wait_recv()
            z_u(s, way, ubuf.at[t, s, p]).wait_recv()

            @pl.when(onward)
            def _():
                z_d(s, way, dbuf.at[t, s]).start()
                z_u(s, way, ubuf.at[t, s, p]).start()

            for i in range(1, tenant):
                x_d(s, i, dbuf.at[t, s]).start()

    def across(k, way):
        s, fine, _ = place(k, way)
        if shares > 1:

            @pl.when(fine)
            def _():
                other = g * shares + lax.rem(side_t, shares)
                remote(
                    wbuf.at[s, other], wbuf.at[s, other], xw_s.at[s], xw_r.at[s], tenant=side_t
                ).wait_recv()
                for i in range(1, groups):
                    y_w(s, i, lax.rem(side_t, shares)).start()

    def finish(k, way):
        s, fine, _ = place(k, way)

        @pl.when(fine)
        def _():
            for i in range(1, tenant):
                x_d_in(s, i).wait_recv()
            for i in range(1, groups):
                for which in range(shares):
                    y_w_in(s, i, which).wait_recv()
            multiply(s)

    def pipeline(n, carry):
        k, way = n // 2 + 1, lax.rem(n, 2)
        relay(k, way)
        across(k - 1, way)
        finish(k - 2, way)
        return carry

    lax.fori_loop(0, 2 * (fsdp - 1), pipeline, 0)

    core_u = remote(ubuf.at[t, :, p], ubuf.at[t, :, p], cu_s, cu_r, pair=1 - p)
    core_u.start()

    def tail(n, carry):
        k, way = n // 2 + 1, lax.rem(n, 2)
        across(k - 1, way)
        finish(k - 2, way)
        return carry

    lax.fori_loop(2 * (fsdp - 1), 2 * fsdp, tail, 0)
    core_u.wait_send()
    remote(ubuf.at[t, :, 1 - p], ubuf.at[t, :, 1 - p], cu_s, cu_r, pair=1 - p).wait_recv()

    def x_u(i):
        return remote(
            ubuf.at[t], ubuf.at[t], xu_s.at[i], xu_r.at[t], tenant=lax.rem(t + i, tenant)
        )

    for i in range(1, tenant):
        x_u(i).start()
    lax.fori_loop(2 * fsdp, 2 * (fsdp + 1), tail, 0)

    sends = [
        remote(acc.at[1], pacc, part_s.at[0], part_r.at[0], pair=1 - p),
        remote(lacc.at[1], placc, part_s.at[1], part_r.at[1], pair=1 - p),
    ]
    for copy in sends:
        copy.start()
    for i in range(1, tenant):
        other = lax.rem(t + i, tenant)
        remote(ubuf.at[other], ubuf.at[other], xu_s.at[i], xu_r.at[other], tenant=other).wait_recv()
    for copy in sends:
        copy.wait_recv()

    outs = acc.shape[2]

    def up_map(m):
        return ubuf[m].reshape(outs, lanes)

    def choice(where):
        span = where.shape[1]
        row = lax.broadcasted_iota(jnp.int32, (lanes, span), 0)
        col = lax.broadcasted_iota(jnp.int32, (lanes, span), 1)
        mark = jnp.where(row < rank, where[0:1], where[1:2])
        return jnp.where((row & (rank - 1)) == (col & (rank - 1)), mark, 0.0)

    mine = choice(marks[...]).astype(BF16)
    sign = 1.0 - 2.0 * p.astype(F32)
    position = lax.broadcasted_iota(jnp.int32, (block, 1), 0).astype(F32)
    lane = lax.broadcasted_iota(jnp.int32, (block, lanes), 1)
    score[...] = jnp.zeros_like(score)
    weights = readout[...]

    for j in range(slots):
        rows = pl.ds(j * block, block)
        low = ((lacc[0, rows] + placc[rows]) * marks[j : j + 1]).astype(BF16)
        lowm[rows] = low
        mixed = acc[0, rows] + pacc[rows]
        for m in range(tenant):
            mixed += dot(low[:, m * lanes : (m + 1) * lanes], up_map(m), NT)
        acc[0, rows] = mixed
        gate = jax.nn.sigmoid(mixed)
        each = jnp.sum(weights * (mixed * gate), axis=1, keepdims=True)
        valid = (position < scalars[j]).astype(F32)
        total = jnp.sum(each * valid, axis=0, keepdims=True)
        score[j : j + 1] = jnp.broadcast_to(total, (1, score.shape[1]))
    swap = remote(score, pscore, score_s, score_r, pair=1 - p)
    swap.start()
    swap.wait_recv()

    rising = jnp.zeros((lanes, outs), F32)
    loss_out[...] = jnp.zeros_like(loss_out)
    for j in range(slots):
        rows = pl.ds(j * block, block)
        logit = BETA * (sign * (score[j : j + 1] - pscore[j : j + 1]) - scalars[2 + j])
        alive = scalars[4 + j]
        down_side = -logit
        plus = jnp.maximum(down_side, 0.0) + jnp.log1p(jnp.exp(-jnp.abs(down_side)))
        loss_out[j : j + 1] = alive * plus
        factor = (-BETA * alive * sign) * jax.nn.sigmoid(down_side)
        valid = (position < scalars[j]).astype(F32)
        mixed = acc[0, rows]
        gate = jax.nn.sigmoid(mixed)
        slope = gate * (1.0 + mixed * (1.0 - gate))
        turn = ((factor[:, :1] * valid) * weights * slope).astype(BF16)
        cot[rows] = turn
        small = jnp.zeros((block, lanes), F32)
        kept = jnp.zeros((block, lanes), F32)
        for m in range(tenant):
            span = slice(m * lanes, (m + 1) * lanes)
            grad = (dot(turn, up_map(m)) * marks[j : j + 1, span]).astype(BF16)
            small += dot(grad, mine[:, span], NT)
            kept += dot(lowm[rows, span], mine[:, span], NT)
        inside = (lane >= j * rank) & (lane < (j + 1) * rank)
        small = jnp.where(inside, small, 0.0)
        kept = jnp.where(inside, kept, 0.0)
        lgt[0, :, rows] = small.T.astype(BF16)
        rising += dot(kept.T.astype(BF16), turn)
    upsum[...] = rising.T.reshape(upsum.shape)
    mids = [
        remote(lgt.at[0], lgt.at[1], mid_s.at[0], mid_r.at[0], pair=1 - p),
        remote(upsum.at[:, 1 - p], upeer, mid_s.at[1], mid_r.at[1], pair=1 - p),
    ]
    for copy in mids:
        copy.start()

    def z_p(i):
        other = lax.rem(f + i, fsdp)
        return remote(ps.at[other], pr.at[f], p_s.at[i], p_r.at[f], fsdp=other)

    def z_q(i):
        other = lax.rem(f + i, fsdp)
        return remote(uz.at[other], ur.at[f], q_s.at[i], q_r.at[f], fsdp=other)

    mids[0].wait_recv()

    def share(s):
        return (dot(lgt[0], tokens[0, s]) + dot(lgt[1], tokens[1, s])).astype(BF16)

    def send_share(i, carry):
        s = lax.rem(f + i, fsdp)
        ps[s] = share(s)
        z_p(i).start()
        return carry

    lax.fori_loop(1, fsdp, send_share, 0)
    mids[1].wait_recv()
    for s in range(fsdp):
        uz[s] = (upsum[s, p] + upeer[s]).astype(BF16)
    for i in range(1, fsdp):
        z_q(i).start()
    pr[f] = share(f)
    ur[f] = uz[f]
    for i in range(1, fsdp):
        z_mark_in(i).wait_recv()
        other = lax.rem(f + i, fsdp)
        remote(ps.at[other], pr.at[other], p_s.at[i], p_r.at[other], fsdp=other).wait_recv()
        remote(uz.at[other], ur.at[other], q_s.at[i], q_r.at[other], fsdp=other).wait_recv()

    def gathered(m):
        at = pl.ds(pl.multiple_of(m * lanes, lanes), lanes)

        def add(s, carry):
            big, little = carry
            pick = choice(mbuf[s, :, at])
            big += dot(pick.T.astype(BF16), pr[s])
            little += dot(ur[s], pick.astype(BF16))
            return big, little

        zero = (jnp.zeros((lanes, width), F32), jnp.zeros((ur.shape[1], lanes), F32))
        return lax.fori_loop(0, fsdp, add, zero)

    outward = []
    for i in range(1, tenant):
        other = lax.rem(t + i, tenant)
        big, little = gathered(other)
        xs[i] = big.astype(BF16)
        xus[i] = little.astype(BF16)
        outward.append(remote(xs.at[i], xr.at[i], xg_s.at[0, i], xg_r.at[0, i], tenant=other))
        outward.append(remote(xus.at[i], xur.at[i], xg_s.at[1, i], xg_r.at[1, i], tenant=other))
        outward[-2].start()
        outward[-1].start()
    big, little = gathered(t)
    for copy in outward:
        copy.wait()
    for i in range(1, tenant):
        big += xr[i].astype(F32)
        little += xur[i].astype(F32)
    down_out[...] = big.astype(BF16)
    up_out[...] = little.astype(BF16)

    for way in (0, 1):

        @pl.when((f < fsdp - 1) if way == 0 else (f > 0))
        def _():
            z_w(f, way, base.at[quarter]).wait_send()
            z_d(f, way, down).wait_send()
            z_u(f, way, up).wait_send()

    for i in range(1, tenant):
        x_d(f, i, down).wait_send()
        x_u(i).wait_send()
    core_tokens(f).wait_send()

    def left(i, carry):
        core_tokens(lax.rem(f + i, fsdp)).wait_send()
        z_mark(i).wait_send()
        z_p(i).wait_send()
        z_q(i).wait_send()
        return carry

    lax.fori_loop(1, fsdp, left, 0)

    def passed(n, carry):
        way = lax.rem(n, 2)
        s, fine, onward = place(n // 2 + 1, way)

        @pl.when(onward)
        def _():
            z_w(s, way, wbuf.at[s, quarter]).wait_send()
            z_d(s, way, dbuf.at[t, s]).wait_send()
            z_u(s, way, ubuf.at[t, s, p]).wait_send()

        @pl.when(fine)
        def _():
            if shares > 1:
                x_w(s).wait_send()
            for i in range(1, groups):
                for which in range(shares):
                    y_w(s, i, which).wait_send()
            for i in range(1, tenant):
                x_d(s, i, dbuf.at[t, s]).wait_send()

        return carry

    lax.fori_loop(0, 2 * (fsdp - 1), passed, 0)
    for copy in sends + [swap] + mids:
        copy.wait_send()


def shards(
    hidden,
    pair_adapter_index,
    live_block_count,
    lengths,
    adapter_storage_row,
    frozen_base_weight,
    adapter_down_maps,
    adapter_up_maps,
    readout,
    reference_score_margin,
):
    groups, fsdp = lax.axis_size("groups"), lax.axis_size("fsdp")
    tenant, pair = lax.axis_size("tenant"), lax.axis_size("pair")
    shares = 2 if tenant % 2 == 0 else 1
    _, slots, block, feature = hidden.shape
    held, width, rank = adapter_down_maps.shape
    outs = frozen_base_weight.shape[1]
    up_rows = adapter_up_maps.shape[1]
    adapters = adapter_storage_row.shape[0]
    lanes = slots * rank
    assert held == slots and pair == 2 and slots == 2
    parts = groups * shares
    count = slots * block

    catalog = jnp.arange(adapters, dtype=jnp.int32)
    row = jnp.sum(
        jnp.where(pair_adapter_index[:, None] == catalog[None, :], adapter_storage_row[None, :], 0),
        axis=1,
    )
    marks = (row[:, None] == (jnp.arange(adapters * rank) // rank)[None, :]).astype(F32)
    marks = jnp.pad(marks, ((0, 8 - slots), (0, 0)))
    alive = (jnp.arange(slots, dtype=jnp.int32) < live_block_count[0]).astype(F32)
    scalars = jnp.concatenate(
        [lengths[0].astype(F32), reference_score_margin, alive, jnp.zeros((2,), F32)]
    )
    base = frozen_base_weight.reshape(parts, width // parts, outs)
    down = adapter_down_maps.transpose(0, 2, 1).reshape(lanes, width)
    up = adapter_up_maps.transpose(1, 0, 2).reshape(up_rows, lanes)
    flat = hidden.reshape(count, feature)

    def kernel(scal, read, mark, hid, *refs):
        view = BlockView(hid, width)
        step_kernel((groups, fsdp, tenant, shares, rank), scal, read, mark, view, *refs)

    any_space = pl.BlockSpec(memory_space=pl.ANY)
    vmem = pl.BlockSpec(memory_space=pltpu.VMEM)
    span = tenant * lanes
    dma = pltpu.SemaphoreType.DMA
    loss, down_grad, up_grad = pl.pallas_call(
        kernel,
        out_shape=(
            jax.ShapeDtypeStruct((8, 128), F32),
            jax.ShapeDtypeStruct((lanes, width), BF16),
            jax.ShapeDtypeStruct((up_rows, lanes), BF16),
        ),
        in_specs=[pl.BlockSpec(memory_space=pltpu.SMEM), vmem, vmem] + [any_space] * 4,
        out_specs=(vmem, vmem, vmem),
        scratch_shapes=[
            pltpu.VMEM((2, fsdp, count, width), BF16),
            pltpu.VMEM((fsdp, parts, width // parts, outs), BF16),
            pltpu.VMEM((tenant, fsdp, lanes, width), BF16),
            pltpu.VMEM((tenant, fsdp, 2, up_rows, lanes), BF16),
            pltpu.VMEM((fsdp, 8, span), F32),
            pltpu.VMEM((2, count, outs), F32),
            pltpu.VMEM((2, count, span), F32),
            pltpu.VMEM((count, outs), F32),
            pltpu.VMEM((count, span), F32),
            pltpu.VMEM((8, 128), F32),
            pltpu.VMEM((8, 128), F32),
            pltpu.VMEM((count, span), BF16),
            pltpu.VMEM((count, outs), BF16),
            pltpu.VMEM((2, lanes, count), BF16),
            pltpu.VMEM((fsdp, 2, up_rows, lanes), F32),
            pltpu.VMEM((fsdp, up_rows, lanes), F32),
            pltpu.VMEM((fsdp, up_rows, lanes), BF16),
            pltpu.VMEM((fsdp, up_rows, lanes), BF16),
            pltpu.VMEM((fsdp, lanes, width), BF16),
            pltpu.VMEM((fsdp, lanes, width), BF16),
            pltpu.VMEM((tenant, lanes, width), BF16),
            pltpu.VMEM((tenant, lanes, width), BF16),
            pltpu.VMEM((tenant, up_rows, lanes), BF16),
            pltpu.VMEM((tenant, up_rows, lanes), BF16),
            dma((fsdp,)), dma((3,)), dma((fsdp,)), dma((fsdp,)),
            dma((fsdp, 2)), dma((fsdp,)), dma((fsdp, 2)), dma((fsdp,)),
            dma((fsdp, 2)), dma((fsdp,)), dma((fsdp,)), dma((fsdp,)),
            dma((fsdp,)), dma((fsdp,)), dma((fsdp, tenant)), dma((tenant, fsdp)),
            dma((fsdp, groups, shares)), dma((fsdp, parts)),
            dma(()), dma(()), dma((tenant,)), dma((tenant,)),
            dma((2,)), dma((2,)), dma(()), dma(()), dma((2,)), dma((2,)),
            dma((fsdp,)), dma((fsdp,)), dma((fsdp,)), dma((fsdp,)),
            dma((2, tenant)), dma((2, tenant)),
        ],
        compiler_params=pltpu.CompilerParams(
            collective_id=0, has_side_effects=True, vmem_limit_bytes=48 * 1024 * 1024
        ),
        cost_estimate=pl.CostEstimate(
            flops=4 * count * feature * (outs + 2 * span), bytes_accessed=8 << 20, transcendentals=0
        ),
    )(scalars, readout.reshape(1, outs), marks, flat, base, down, up)
    down_gradient = down_grad.reshape(held, rank, width).transpose(0, 2, 1)
    up_gradient = up_grad.reshape(up_rows, held, rank).transpose(1, 0, 2)
    return loss[:slots, 0], down_gradient, up_gradient


class BlockView:
    def __init__(self, ref, width):
        self.ref, self.width = ref, width
        self.at = self

    def __getitem__(self, where):
        s, p = where
        start = pl.multiple_of((s * 2 + p) * self.width, self.width)
        return self.ref.at[:, pl.ds(start, self.width)]


def solution(mesh):
    return jax.shard_map(
        shards,
        mesh=mesh,
        in_specs=(
            P("pair", ("groups", "fsdp", "tenant"), None, None),
            P(("groups", "fsdp", "tenant")),
            P(("groups", "fsdp", "tenant")),
            P("pair", ("groups", "fsdp", "tenant")),
            P(),
            P(("fsdp", "pair"), None),
            P("tenant", ("fsdp", "pair"), None),
            P("tenant", ("fsdp", "pair"), None),
            P(),
            P(("groups", "fsdp", "tenant")),
        ),
        out_specs=(
            P(("groups", "fsdp", "tenant")),
            P(("groups", "tenant"), ("fsdp", "pair"), None),
            P(("groups", "tenant"), ("fsdp", "pair"), None),
        ),
        check_vma=False,
    )
```

```python
import jax
import jax.numpy as jnp
from jax import lax
from jax.experimental import pallas as pl
from jax.experimental.pallas import tpu as pltpu
from jax.sharding import PartitionSpec as P

BETA = 0.01
F32, BF16 = jnp.float32, jnp.bfloat16
NN = (((1,), (0,)), ((), ()))
NT = (((1,), (1,)), ((), ()))


def dot(a, b, dims=NN):
    return lax.dot_general(a, b, dims, preferred_element_type=F32)


def step_kernel(
    sizes,
    index, live, lengths, storage, margins, readout, up, hidden, base, down,
    loss_out, down_out, up_out,
    marks, tokens, wbuf, dbuf, ubuf, mbuf, acc, lacc, pacc, placc,
    score, pscore, lowm, cot, lgt, upsum, upeer, uz, ur, ps, pr, xs, xr, xus, xur,
    loc, locw, tok_s, tok_r, zw_s, zw_r, zd_s, zd_r, zu_s, zu_r, zm_s, zm_r,
    xw_s, xw_r, xd_s, xd_r, yw_s, yw_r, cu_s, cu_r, xu_s, xu_r,
    part_s, part_r, score_s, score_r, mid_s, mid_r, p_s, p_r, q_s, q_r, xg_s, xg_r,
):
    groups, fsdp, tenant, shares, rank = sizes
    g, f = lax.axis_index("groups"), lax.axis_index("fsdp")
    t, p = lax.axis_index("tenant"), lax.axis_index("pair")
    chunks = ps.shape[0]
    slots, block = 2, tokens.shape[2] // 2
    width = tokens.shape[3]
    lanes = slots * rank
    quarter = g * shares + lax.rem(t, shares)
    side_t = t + 1 - 2 * lax.rem(t, 2)

    def remote(src, dst, send, recv, **where):
        return pltpu.make_async_remote_copy(
            src_ref=src, dst_ref=dst, send_sem=send, recv_sem=recv,
            device_id=where, device_id_type=pl.DeviceIdType.MESH,
        )

    barrier = pltpu.get_barrier_semaphore()
    others = [{"pair": 1 - p}]
    others += [{"fsdp": lax.rem(f + i, fsdp)} for i in range(1, fsdp)]
    others += [{"tenant": lax.rem(t + i, tenant)} for i in range(1, tenant)]
    others += [{"groups": lax.rem(g + i, groups)} for i in range(1, groups)]
    for where in others:
        pl.semaphore_signal(barrier, 1, device_id=where, device_id_type=pl.DeviceIdType.MESH)

    def own_tokens(s):
        return pltpu.make_async_copy(hidden.at[s, p], tokens.at[0, s], loc.at[s])

    local = [
        pltpu.make_async_copy(base, wbuf.at[f], locw.at[0]),
        pltpu.make_async_copy(down, dbuf.at[t, f], locw.at[1]),
    ]
    for copy in local:
        copy.start()
    own_tokens(f).start()
    span = marks.shape[1]
    marks[...] = jnp.zeros_like(marks)
    for j in range(slots):
        held = jnp.int32(0)
        for a in range(storage.shape[0]):
            held += jnp.where(index[j] == a, storage[a], 0)
        first = lax.broadcasted_iota(jnp.int32, (1, span), 1) - held * rank
        marks[j : j + 1] = jnp.where((first >= 0) & (first < rank), 1.0, 0.0)
    mbuf[f] = marks[...]
    ubuf[t, f, p] = jnp.concatenate([up[a] for a in range(up.shape[0])], axis=1)
    pl.semaphore_wait(barrier, len(others))

    def to_z(s, way):
        return {"fsdp": f + 1 - 2 * way}

    def z_w(s, way, src):
        return remote(src, wbuf.at[s, quarter], zw_s.at[s, way], zw_r.at[s], **to_z(s, way))

    def z_d(s, way, src):
        return remote(src, dbuf.at[t, s], zd_s.at[s, way], zd_r.at[s], **to_z(s, way))

    def z_u(s, way, src):
        return remote(src, ubuf.at[t, s, p], zu_s.at[s, way], zu_r.at[s], **to_z(s, way))

    def x_w(s):
        return remote(
            wbuf.at[s, quarter], wbuf.at[s, quarter], xw_s.at[s], xw_r.at[s], tenant=side_t
        )

    def x_d(s, i, src):
        return remote(
            src, dbuf.at[t, s], xd_s.at[s, i], xd_r.at[t, s], tenant=lax.rem(t + i, tenant)
        )

    def x_d_in(s, i):
        other = lax.rem(t + i, tenant)
        return remote(
            dbuf.at[other, s], dbuf.at[other, s], xd_s.at[s, i], xd_r.at[other, s], tenant=other
        )

    def y_w(s, i, which):
        row = g * shares + which
        return remote(
            wbuf.at[s, row], wbuf.at[s, row], yw_s.at[s, i, which], yw_r.at[s, row],
            groups=lax.rem(g + i, groups),
        )

    def y_w_in(s, i, which):
        other = lax.rem(g + i, groups)
        row = other * shares + which
        return remote(
            wbuf.at[s, row], wbuf.at[s, row], yw_s.at[s, i, which], yw_r.at[s, row], groups=other
        )

    def core_tokens(s):
        return remote(
            hidden.at[s, 1 - p], tokens.at[1, s], tok_s.at[s], tok_r.at[s], pair=1 - p
        )

    def z_mark(i):
        return remote(
            mbuf.at[f], mbuf.at[f], zm_s.at[i], zm_r.at[f], fsdp=lax.rem(f + i, fsdp)
        )

    def z_mark_in(i):
        other = lax.rem(f + i, fsdp)
        return remote(mbuf.at[other], mbuf.at[other], zm_s.at[i], zm_r.at[other], fsdp=other)

    for way in (0, 1):

        @pl.when((f < fsdp - 1) if way == 0 else (f > 0))
        def _():
            z_w(f, way, base.at[quarter]).start()
            z_d(f, way, down).start()
            z_u(f, way, ubuf.at[t, f, p]).start()

    for i in range(1, tenant):
        x_d(f, i, down).start()
    core_tokens(f).start()

    def rest(i, carry):
        s = lax.rem(f + i, fsdp)
        own_tokens(s).start()
        core_tokens(s).start()
        return carry

    lax.fori_loop(1, fsdp, rest, 0)
    for i in range(1, fsdp):
        z_mark(i).start()
    acc[...] = jnp.zeros_like(acc)
    lacc[...] = jnp.zeros_like(lacc)
    for copy in local:
        copy.wait()

    column = 256

    def multiply(s):
        own_tokens(s).wait()
        core_tokens(s).wait_recv()
        rows = wbuf.shape[1] * wbuf.shape[2]

        def half(h, carry):
            def columns(c, inner):
                at = pl.ds(pl.multiple_of(c * column, column), column)
                weight = wbuf[s, :, :, at].reshape(rows, column)
                acc[h, :, at] += dot(tokens[h, s], weight)
                return inner

            lax.fori_loop(0, wbuf.shape[3] // column, columns, 0)

            def maps(m, inner):
                at = pl.ds(pl.multiple_of(m * lanes, lanes), lanes)
                lacc[h, :, at] += dot(tokens[h, s], dbuf[m, s], NT)
                return inner

            lax.fori_loop(0, tenant, maps, 0)
            return carry

        lax.fori_loop(0, 2, half, 0)

    for i in range(1, tenant):
        x_d_in(f, i).wait_recv()
    multiply(f)

    def place(k, way):
        s = jnp.where(way == 0, f - k, f + k)
        fine = (k >= 1) & (k < fsdp) & (s >= 0) & (s < fsdp)
        onward = fine & jnp.where(way == 0, f < fsdp - 1, f > 0)
        return jnp.clip(s, 0, fsdp - 1), fine, onward

    def relay_base(k, way):
        s, fine, onward = place(k, way)

        @pl.when(fine)
        def _():
            z_w(s, way, wbuf.at[s, quarter]).wait_recv()

            @pl.when(onward)
            def _():
                z_w(s, way, wbuf.at[s, quarter]).start()

            if shares > 1:
                x_w(s).start()
            for i in range(1, groups):
                y_w(s, i, lax.rem(t, shares)).start()

    def relay_maps(k, way):
        s, fine, onward = place(k, way)

        @pl.when(fine)
        def _():
            z_d(s, way, dbuf.at[t, s]).wait_recv()

            @pl.when(onward)
            def _():
                z_d(s, way, dbuf.at[t, s]).start()

            for i in range(1, tenant):
                x_d(s, i, dbuf.at[t, s]).start()
            z_u(s, way, ubuf.at[t, s, p]).wait_recv()

            @pl.when(onward)
            def _():
                z_u(s, way, ubuf.at[t, s, p]).start()

    def across(k, way):
        s, fine, _ = place(k, way)
        if shares > 1:

            @pl.when(fine)
            def _():
                other = g * shares + lax.rem(side_t, shares)
                remote(
                    wbuf.at[s, other], wbuf.at[s, other], xw_s.at[s], xw_r.at[s], tenant=side_t
                ).wait_recv()
                for i in range(1, groups):
                    y_w(s, i, lax.rem(side_t, shares)).start()

    def finish(k, way):
        s, fine, _ = place(k, way)

        @pl.when(fine)
        def _():
            for i in range(1, tenant):
                x_d_in(s, i).wait_recv()
            for i in range(1, groups):
                for which in range(shares):
                    y_w_in(s, i, which).wait_recv()
            multiply(s)

    def pipeline(k, carry):
        for stage in (relay_base, relay_maps, across):
            for way in (0, 1):
                stage(k, way)

        @pl.when(k < fsdp - 1)
        def _():
            lax.fori_loop(0, 2, lambda way, none: finish(k, way), None)

        return carry

    lax.fori_loop(1, fsdp, pipeline, 0)

    core_u = remote(ubuf.at[t, :, p], ubuf.at[t, :, p], cu_s, cu_r, pair=1 - p)
    core_u.start()
    core_u.wait_send()
    remote(ubuf.at[t, :, 1 - p], ubuf.at[t, :, 1 - p], cu_s, cu_r, pair=1 - p).wait_recv()

    def x_u(i):
        return remote(
            ubuf.at[t], ubuf.at[t], xu_s.at[i], xu_r.at[t], tenant=lax.rem(t + i, tenant)
        )

    for i in range(1, tenant):
        x_u(i).start()
    lax.fori_loop(0, 2, lambda way, none: finish(fsdp - 1, way), None)

    sends = [
        remote(acc.at[1], pacc, part_s.at[0], part_r.at[0], pair=1 - p),
        remote(lacc.at[1], placc, part_s.at[1], part_r.at[1], pair=1 - p),
    ]
    for copy in sends:
        copy.start()
    for i in range(1, tenant):
        other = lax.rem(t + i, tenant)
        remote(ubuf.at[other], ubuf.at[other], xu_s.at[i], xu_r.at[other], tenant=other).wait_recv()
    for copy in sends:
        copy.wait_recv()

    outs = acc.shape[2]

    def up_map(m):
        return ubuf[m].reshape(outs, lanes)

    def choice(where):
        span = where.shape[1]
        row = lax.broadcasted_iota(jnp.int32, (lanes, span), 0)
        col = lax.broadcasted_iota(jnp.int32, (lanes, span), 1)
        mark = jnp.where(row < rank, where[0:1], where[1:2])
        return jnp.where((row & (rank - 1)) == (col & (rank - 1)), mark, 0.0)

    mine = choice(marks[...]).astype(BF16)
    sign = 1.0 - 2.0 * p.astype(F32)
    position = lax.broadcasted_iota(jnp.int32, (block, 1), 0).astype(F32)
    lane = lax.broadcasted_iota(jnp.int32, (block, lanes), 1)
    score[...] = jnp.zeros_like(score)
    weights = readout[...]

    for j in range(slots):
        rows = pl.ds(j * block, block)
        low = ((lacc[0, rows] + placc[rows]) * marks[j : j + 1]).astype(BF16)
        lowm[rows] = low
        mixed = acc[0, rows] + pacc[rows]
        for m in range(tenant):
            mixed += dot(low[:, m * lanes : (m + 1) * lanes], up_map(m), NT)
        acc[0, rows] = mixed
        gate = jax.nn.sigmoid(mixed)
        each = jnp.sum(weights * (mixed * gate), axis=1, keepdims=True)
        valid = (position < lengths[0, j].astype(F32)).astype(F32)
        total = jnp.sum(each * valid, axis=0, keepdims=True)
        score[j : j + 1] = jnp.broadcast_to(total, (1, score.shape[1]))
    swap = remote(score, pscore, score_s, score_r, pair=1 - p)
    swap.start()
    swap.wait_recv()

    rising = jnp.zeros((lanes, outs), F32)
    for j in range(slots):
        rows = pl.ds(j * block, block)
        logit = BETA * (sign * (score[j : j + 1] - pscore[j : j + 1]) - margins[j])
        alive = jnp.where(live[0] > j, 1.0, 0.0)
        down_side = -logit
        plus = jnp.maximum(down_side, 0.0) + jnp.log1p(jnp.exp(-jnp.abs(down_side)))
        loss_out[j] = (alive * plus)[0, 0]
        factor = (-BETA * alive * sign) * jax.nn.sigmoid(down_side)
        valid = (position < lengths[0, j].astype(F32)).astype(F32)
        mixed = acc[0, rows]
        gate = jax.nn.sigmoid(mixed)
        slope = gate * (1.0 + mixed * (1.0 - gate))
        turn = ((factor[:, :1] * valid) * weights * slope).astype(BF16)
        cot[rows] = turn
        small = jnp.zeros((block, lanes), F32)
        kept = jnp.zeros((block, lanes), F32)
        for m in range(tenant):
            span = slice(m * lanes, (m + 1) * lanes)
            grad = (dot(turn, up_map(m)) * marks[j : j + 1, span]).astype(BF16)
            small += dot(grad, mine[:, span], NT)
            kept += dot(lowm[rows, span], mine[:, span], NT)
        inside = (lane >= j * rank) & (lane < (j + 1) * rank)
        small = jnp.where(inside, small, 0.0)
        kept = jnp.where(inside, kept, 0.0)
        lgt[0, :, rows] = small.T.astype(BF16)
        rising += dot(kept.T.astype(BF16), turn)
    upsum[...] = rising.T.reshape(upsum.shape)
    mids = [
        remote(lgt.at[0], lgt.at[1], mid_s.at[0], mid_r.at[0], pair=1 - p),
        remote(upsum.at[:, 1 - p], upeer, mid_s.at[1], mid_r.at[1], pair=1 - p),
    ]
    for copy in mids:
        copy.start()

    part = ps.shape[3]

    def z_p(i, c):
        other = lax.rem(f + i, fsdp)
        return remote(ps.at[c, other], pr.at[c, f], p_s.at[c, i], p_r.at[c, f], fsdp=other)

    def z_p_in(i, c):
        other = lax.rem(f + i, fsdp)
        return remote(
            ps.at[c, other], pr.at[c, other], p_s.at[c, i], p_r.at[c, other], fsdp=other
        )

    def z_q(i):
        other = lax.rem(f + i, fsdp)
        return remote(uz.at[other], ur.at[f], q_s.at[i], q_r.at[f], fsdp=other)

    mids[0].wait_recv()

    def share(s, c):
        at = pl.ds(c * part, part)
        return (dot(lgt[0], tokens[0, s, :, at]) + dot(lgt[1], tokens[1, s, :, at])).astype(BF16)

    def send_share(c):
        def one(i, carry):
            s = lax.rem(f + i, fsdp)
            ps[c, s] = share(s, c)
            z_p(i, c).start()
            return carry

        lax.fori_loop(1, fsdp, one, 0)

    send_share(0)
    mids[1].wait_recv()
    for s in range(fsdp):
        uz[s] = (upsum[s, p] + upeer[s]).astype(BF16)
    for i in range(1, fsdp):
        z_q(i).start()
    for c in range(1, chunks):
        send_share(c)
    for c in range(chunks):
        pr[c, f] = share(f, c)
    ur[f] = uz[f]
    for i in range(1, fsdp):
        z_mark_in(i).wait_recv()

    def pick(m, s):
        at = pl.ds(pl.multiple_of(m * lanes, lanes), lanes)
        return choice(mbuf[s, :, at])

    def gathered(m, c):
        def add(s, big):
            return big + dot(pick(m, s).T.astype(BF16), pr[c, s])

        return lax.fori_loop(0, fsdp, add, jnp.zeros((lanes, part), F32))

    def gathered_up(m):
        def add(s, little):
            return little + dot(ur[s], pick(m, s).astype(BF16))

        return lax.fori_loop(0, fsdp, add, jnp.zeros((ur.shape[1], lanes), F32))

    outward = {}

    def send_down(c):
        for i in range(1, fsdp):
            z_p_in(i, c).wait_recv()
        for i in range(1, tenant):
            other = lax.rem(t + i, tenant)
            xs[c, i] = gathered(other, c).astype(BF16)
            copy = remote(xs.at[c, i], xr.at[c, i], xg_s.at[c, i], xg_r.at[c, i], tenant=other)
            copy.start()
            outward[c, i] = copy

    send_down(0)
    for i in range(1, fsdp):
        other = lax.rem(f + i, fsdp)
        remote(uz.at[other], ur.at[other], q_s.at[i], q_r.at[other], fsdp=other).wait_recv()
    for i in range(1, tenant):
        other = lax.rem(t + i, tenant)
        xus[i] = gathered_up(other).astype(BF16)
        copy = remote(xus.at[i], xur.at[i], xg_s.at[chunks, i], xg_r.at[chunks, i], tenant=other)
        copy.start()
        outward[chunks, i] = copy
    little = gathered_up(t)
    for c in range(1, chunks):
        send_down(c)
    for c in range(chunks):
        big = gathered(t, c)
        for i in range(1, tenant):
            outward[c, i].wait_recv()
            big += xr[c, i].astype(F32)
        down_out[:, pl.ds(c * part, part)] = big.astype(BF16)
    for i in range(1, tenant):
        outward[chunks, i].wait_recv()
        little += xur[i].astype(F32)
    for a in range(up_out.shape[0]):
        up_out[a] = little[:, a * rank : (a + 1) * rank].astype(BF16)
    for copy in outward.values():
        copy.wait_send()

    for way in (0, 1):

        @pl.when((f < fsdp - 1) if way == 0 else (f > 0))
        def _():
            z_w(f, way, base.at[quarter]).wait_send()
            z_d(f, way, down).wait_send()
            z_u(f, way, ubuf.at[t, f, p]).wait_send()

    for i in range(1, tenant):
        x_d(f, i, down).wait_send()
        x_u(i).wait_send()
    core_tokens(f).wait_send()

    def left(i, carry):
        core_tokens(lax.rem(f + i, fsdp)).wait_send()
        z_mark(i).wait_send()
        for c in range(chunks):
            z_p(i, c).wait_send()
        z_q(i).wait_send()
        return carry

    lax.fori_loop(1, fsdp, left, 0)

    def passed(n, carry):
        way = lax.rem(n, 2)
        s, fine, onward = place(n // 2 + 1, way)

        @pl.when(onward)
        def _():
            z_w(s, way, wbuf.at[s, quarter]).wait_send()
            z_d(s, way, dbuf.at[t, s]).wait_send()
            z_u(s, way, ubuf.at[t, s, p]).wait_send()

        @pl.when(fine)
        def _():
            if shares > 1:
                x_w(s).wait_send()
            for i in range(1, groups):
                for which in range(shares):
                    y_w(s, i, which).wait_send()
            for i in range(1, tenant):
                x_d(s, i, dbuf.at[t, s]).wait_send()

        return carry

    lax.fori_loop(0, 2 * (fsdp - 1), passed, 0)
    for copy in sends + [swap] + mids:
        copy.wait_send()


def shards(
    hidden,
    pair_adapter_index,
    live_block_count,
    lengths,
    adapter_storage_row,
    frozen_base_weight,
    adapter_down_maps,
    adapter_up_maps,
    readout,
    reference_score_margin,
):
    groups, fsdp = lax.axis_size("groups"), lax.axis_size("fsdp")
    tenant, pair = lax.axis_size("tenant"), lax.axis_size("pair")
    shares = 2 if tenant % 2 == 0 else 1
    _, slots, block, feature = hidden.shape
    held, width, rank = adapter_down_maps.shape
    outs = frozen_base_weight.shape[1]
    up_rows = adapter_up_maps.shape[1]
    lanes = slots * rank
    assert held == slots and pair == 2 and slots == 2
    parts = groups * shares
    count = slots * block

    base = frozen_base_weight.reshape(parts, width // parts, outs)
    down = adapter_down_maps.transpose(0, 2, 1).reshape(lanes, width)
    flat = hidden.reshape(count, feature)

    def kernel(*refs):
        view = BlockView(refs[7], width)
        step_kernel((groups, fsdp, tenant, shares, rank), *refs[:7], view, *refs[8:])

    any_space = pl.BlockSpec(memory_space=pl.ANY)
    vmem = pl.BlockSpec(memory_space=pltpu.VMEM)
    smem = pl.BlockSpec(memory_space=pltpu.SMEM)
    span = tenant * lanes
    chunks = 2
    dma = pltpu.SemaphoreType.DMA
    loss, down_grad, up_grad = pl.pallas_call(
        kernel,
        out_shape=(
            jax.ShapeDtypeStruct((slots,), F32),
            jax.ShapeDtypeStruct((lanes, width), BF16),
            jax.ShapeDtypeStruct(adapter_up_maps.shape, BF16),
        ),
        in_specs=[smem] * 5 + [vmem, vmem] + [any_space] * 3,
        out_specs=(smem, vmem, vmem),
        scratch_shapes=[
            pltpu.VMEM((8, span), F32),
            pltpu.VMEM((2, fsdp, count, width), BF16),
            pltpu.VMEM((fsdp, parts, width // parts, outs), BF16),
            pltpu.VMEM((tenant, fsdp, lanes, width), BF16),
            pltpu.VMEM((tenant, fsdp, 2, up_rows, lanes), BF16),
            pltpu.VMEM((fsdp, 8, span), F32),
            pltpu.VMEM((2, count, outs), F32),
            pltpu.VMEM((2, count, span), F32),
            pltpu.VMEM((count, outs), F32),
            pltpu.VMEM((count, span), F32),
            pltpu.VMEM((8, 128), F32),
            pltpu.VMEM((8, 128), F32),
            pltpu.VMEM((count, span), BF16),
            pltpu.VMEM((count, outs), BF16),
            pltpu.VMEM((2, lanes, count), BF16),
            pltpu.VMEM((fsdp, 2, up_rows, lanes), F32),
            pltpu.VMEM((fsdp, up_rows, lanes), F32),
            pltpu.VMEM((fsdp, up_rows, lanes), BF16),
            pltpu.VMEM((fsdp, up_rows, lanes), BF16),
            pltpu.VMEM((chunks, fsdp, lanes, width // chunks), BF16),
            pltpu.VMEM((chunks, fsdp, lanes, width // chunks), BF16),
            pltpu.VMEM((chunks, tenant, lanes, width // chunks), BF16),
            pltpu.VMEM((chunks, tenant, lanes, width // chunks), BF16),
            pltpu.VMEM((tenant, up_rows, lanes), BF16),
            pltpu.VMEM((tenant, up_rows, lanes), BF16),
            dma((fsdp,)), dma((2,)), dma((fsdp,)), dma((fsdp,)),
            dma((fsdp, 2)), dma((fsdp,)), dma((fsdp, 2)), dma((fsdp,)),
            dma((fsdp, 2)), dma((fsdp,)), dma((fsdp,)), dma((fsdp,)),
            dma((fsdp,)), dma((fsdp,)), dma((fsdp, tenant)), dma((tenant, fsdp)),
            dma((fsdp, groups, shares)), dma((fsdp, parts)),
            dma(()), dma(()), dma((tenant,)), dma((tenant,)),
            dma((2,)), dma((2,)), dma(()), dma(()), dma((2,)), dma((2,)),
            dma((chunks, fsdp)), dma((chunks, fsdp)), dma((fsdp,)), dma((fsdp,)),
            dma((chunks + 1, tenant)), dma((chunks + 1, tenant)),
        ],
        compiler_params=pltpu.CompilerParams(
            collective_id=0, has_side_effects=True, vmem_limit_bytes=48 * 1024 * 1024
        ),
        cost_estimate=pl.CostEstimate(
            flops=4 * count * feature * (outs + 2 * span), bytes_accessed=8 << 20, transcendentals=0
        ),
    )(
        pair_adapter_index, live_block_count, lengths, adapter_storage_row,
        reference_score_margin, readout.reshape(1, outs), adapter_up_maps, flat, base, down,
    )
    down_gradient = down_grad.reshape(held, rank, width).transpose(0, 2, 1)
    return loss, down_gradient, up_grad


class BlockView:
    def __init__(self, ref, width):
        self.ref, self.width = ref, width
        self.at = self

    def __getitem__(self, where):
        s, p = where
        start = pl.multiple_of((s * 2 + p) * self.width, self.width)
        return self.ref.at[:, pl.ds(start, self.width)]


def solution(mesh):
    return jax.shard_map(
        shards,
        mesh=mesh,
        in_specs=(
            P("pair", ("groups", "fsdp", "tenant"), None, None),
            P(("groups", "fsdp", "tenant")),
            P(("groups", "fsdp", "tenant")),
            P("pair", ("groups", "fsdp", "tenant")),
            P(),
            P(("fsdp", "pair"), None),
            P("tenant", ("fsdp", "pair"), None),
            P("tenant", ("fsdp", "pair"), None),
            P(),
            P(("groups", "fsdp", "tenant")),
        ),
        out_specs=(
            P(("groups", "fsdp", "tenant")),
            P(("groups", "tenant"), ("fsdp", "pair"), None),
            P(("groups", "tenant"), ("fsdp", "pair"), None),
        ),
        check_vma=False,
    )
```

```python
import jax
import jax.numpy as jnp
from jax import lax
from jax.experimental import pallas as pl
from jax.experimental.pallas import tpu as pltpu
from jax.sharding import PartitionSpec as P

BETA = 0.01
F32, BF16 = jnp.float32, jnp.bfloat16
NN = (((1,), (0,)), ((), ()))
NT = (((1,), (1,)), ((), ()))


def dot(a, b, dims=NN):
    return lax.dot_general(a, b, dims, preferred_element_type=F32)


def step_kernel(
    sizes,
    index_in, live_in, lengths_in, storage_in, margins_in, readout_in, up_in, hidden, base, down,
    loss_out, down_out, up_out,
    index, live, lengths, storage, margins, readout, up, small_sem,
    marks, tokens, wbuf, dbuf, ubuf, mbuf, acc, lacc, pacc, placc,
    score, pscore, lowm, cot, lgt, upsum, upeer, uz, ur, ps, pr, xs, xr, xus, xur,
    loc, locw, tok_s, tok_r, zw_s, zw_r, zd_s, zd_r, zu_s, zu_r, zm_s, zm_r,
    xw_s, xw_r, xd_s, xd_r, yw_s, yw_r, cu_s, cu_r, xu_s, xu_r,
    part_s, part_r, score_s, score_r, mid_s, mid_r, p_s, p_r, q_s, q_r, xg_s, xg_r,
):
    groups, fsdp, tenant, shares, rank = sizes
    g, f = lax.axis_index("groups"), lax.axis_index("fsdp")
    t, p = lax.axis_index("tenant"), lax.axis_index("pair")
    chunks = ps.shape[0]
    slots, block = 2, tokens.shape[2] // 2
    width = tokens.shape[3]
    lanes = slots * rank
    quarter = g * shares + lax.rem(t, shares)
    side_t = t + 1 - 2 * lax.rem(t, 2)

    def remote(src, dst, send, recv, **where):
        return pltpu.make_async_remote_copy(
            src_ref=src, dst_ref=dst, send_sem=send, recv_sem=recv,
            device_id=where, device_id_type=pl.DeviceIdType.MESH,
        )

    barrier = pltpu.get_barrier_semaphore()
    others = [{"pair": 1 - p}]
    others += [{"fsdp": lax.rem(f + i, fsdp)} for i in range(1, fsdp)]
    others += [{"tenant": lax.rem(t + i, tenant)} for i in range(1, tenant)]
    others += [{"groups": lax.rem(g + i, groups)} for i in range(1, groups)]
    smalls = [
        pltpu.make_async_copy(src, dst, small_sem.at[i])
        for i, (src, dst) in enumerate(
            zip(
                (index_in, live_in, lengths_in, storage_in, margins_in, readout_in, up_in),
                (index, live, lengths, storage, margins, readout, up),
            )
        )
    ]
    for copy in smalls:
        copy.start()
    for where in others:
        pl.semaphore_signal(barrier, 1, device_id=where, device_id_type=pl.DeviceIdType.MESH)

    def own_tokens(s):
        return pltpu.make_async_copy(hidden.at[s, p], tokens.at[0, s], loc.at[s])

    local = [
        pltpu.make_async_copy(base, wbuf.at[f], locw.at[0]),
        pltpu.make_async_copy(down, dbuf.at[t, f], locw.at[1]),
    ]
    for copy in local:
        copy.start()
    own_tokens(f).start()
    pl.semaphore_wait(barrier, len(others))

    def to_z(s, way):
        return {"fsdp": f + 1 - 2 * way}

    def z_w(s, way, src):
        return remote(src, wbuf.at[s, quarter], zw_s.at[s, way], zw_r.at[s], **to_z(s, way))

    def z_d(s, way, src):
        return remote(src, dbuf.at[t, s], zd_s.at[s, way], zd_r.at[s], **to_z(s, way))

    def z_u(s, way, src):
        return remote(src, ubuf.at[t, s, p], zu_s.at[s, way], zu_r.at[s], **to_z(s, way))

    def x_w(s):
        return remote(
            wbuf.at[s, quarter], wbuf.at[s, quarter], xw_s.at[s], xw_r.at[s], tenant=side_t
        )

    def x_d(s, i, src):
        return remote(
            src, dbuf.at[t, s], xd_s.at[s, i], xd_r.at[t, s], tenant=lax.rem(t + i, tenant)
        )

    def x_d_in(s, i):
        other = lax.rem(t + i, tenant)
        return remote(
            dbuf.at[other, s], dbuf.at[other, s], xd_s.at[s, i], xd_r.at[other, s], tenant=other
        )

    def y_w(s, i, which):
        row = g * shares + which
        return remote(
            wbuf.at[s, row], wbuf.at[s, row], yw_s.at[s, i, which], yw_r.at[s, row],
            groups=lax.rem(g + i, groups),
        )

    def y_w_in(s, i, which):
        other = lax.rem(g + i, groups)
        row = other * shares + which
        return remote(
            wbuf.at[s, row], wbuf.at[s, row], yw_s.at[s, i, which], yw_r.at[s, row], groups=other
        )

    def core_tokens(s):
        return remote(
            hidden.at[s, 1 - p], tokens.at[1, s], tok_s.at[s], tok_r.at[s], pair=1 - p
        )

    def z_mark(i):
        return remote(
            mbuf.at[f], mbuf.at[f], zm_s.at[i], zm_r.at[f], fsdp=lax.rem(f + i, fsdp)
        )

    def z_mark_in(i):
        other = lax.rem(f + i, fsdp)
        return remote(mbuf.at[other], mbuf.at[other], zm_s.at[i], zm_r.at[other], fsdp=other)

    for way in (0, 1):

        @pl.when((f < fsdp - 1) if way == 0 else (f > 0))
        def _():
            z_w(f, way, base.at[quarter]).start()
            z_d(f, way, down).start()

    for i in range(1, tenant):
        x_d(f, i, down).start()
    core_tokens(f).start()

    def rest(i, carry):
        s = lax.rem(f + i, fsdp)
        own_tokens(s).start()
        core_tokens(s).start()
        return carry

    lax.fori_loop(1, fsdp, rest, 0)
    for copy in smalls:
        copy.wait()
    span = marks.shape[1]
    marks[...] = jnp.zeros_like(marks)
    for j in range(slots):
        held = jnp.int32(0)
        for a in range(storage.shape[0]):
            held += jnp.where(index[j] == a, storage[a], 0)
        first = lax.broadcasted_iota(jnp.int32, (1, span), 1) - held * rank
        marks[j : j + 1] = jnp.where((first >= 0) & (first < rank), 1.0, 0.0)
    mbuf[f] = marks[...]
    ubuf[t, f, p] = jnp.concatenate([up[a] for a in range(up.shape[0])], axis=1)
    for way in (0, 1):

        @pl.when((f < fsdp - 1) if way == 0 else (f > 0))
        def _():
            z_u(f, way, ubuf.at[t, f, p]).start()

    for i in range(1, fsdp):
        z_mark(i).start()
    acc[...] = jnp.zeros_like(acc)
    lacc[...] = jnp.zeros_like(lacc)
    for copy in local:
        copy.wait()

    column = 256

    def multiply(s):
        own_tokens(s).wait()
        core_tokens(s).wait_recv()
        rows = wbuf.shape[1] * wbuf.shape[2]

        def half(h, carry):
            def columns(c, inner):
                at = pl.ds(pl.multiple_of(c * column, column), column)
                weight = wbuf[s, :, :, at].reshape(rows, column)
                acc[h, :, at] += dot(tokens[h, s], weight)
                return inner

            lax.fori_loop(0, wbuf.shape[3] // column, columns, 0)

            def maps(m, inner):
                at = pl.ds(pl.multiple_of(m * lanes, lanes), lanes)
                lacc[h, :, at] += dot(tokens[h, s], dbuf[m, s], NT)
                return inner

            lax.fori_loop(0, tenant, maps, 0)
            return carry

        lax.fori_loop(0, 2, half, 0)

    for i in range(1, tenant):
        x_d_in(f, i).wait_recv()
    multiply(f)

    def place(k, way):
        s = jnp.where(way == 0, f - k, f + k)
        fine = (k >= 1) & (k < fsdp) & (s >= 0) & (s < fsdp)
        onward = fine & jnp.where(way == 0, f < fsdp - 1, f > 0)
        return jnp.clip(s, 0, fsdp - 1), fine, onward

    def relay_base(k, way):
        s, fine, onward = place(k, way)

        @pl.when(fine)
        def _():
            z_w(s, way, wbuf.at[s, quarter]).wait_recv()

            @pl.when(onward)
            def _():
                z_w(s, way, wbuf.at[s, quarter]).start()

            if shares > 1:
                x_w(s).start()
            for i in range(1, groups):
                y_w(s, i, lax.rem(t, shares)).start()

    def relay_maps(k, way):
        s, fine, onward = place(k, way)

        @pl.when(fine)
        def _():
            z_d(s, way, dbuf.at[t, s]).wait_recv()

            @pl.when(onward)
            def _():
                z_d(s, way, dbuf.at[t, s]).start()

            for i in range(1, tenant):
                x_d(s, i, dbuf.at[t, s]).start()
            z_u(s, way, ubuf.at[t, s, p]).wait_recv()

            @pl.when(onward)
            def _():
                z_u(s, way, ubuf.at[t, s, p]).start()

    def across(k, way):
        s, fine, _ = place(k, way)
        if shares > 1:

            @pl.when(fine)
            def _():
                other = g * shares + lax.rem(side_t, shares)
                remote(
                    wbuf.at[s, other], wbuf.at[s, other], xw_s.at[s], xw_r.at[s], tenant=side_t
                ).wait_recv()
                for i in range(1, groups):
                    y_w(s, i, lax.rem(side_t, shares)).start()

    def finish(k, way):
        s, fine, _ = place(k, way)

        @pl.when(fine)
        def _():
            for i in range(1, tenant):
                x_d_in(s, i).wait_recv()
            for i in range(1, groups):
                for which in range(shares):
                    y_w_in(s, i, which).wait_recv()
            multiply(s)

    def pipeline(k, carry):
        for stage in (relay_base, relay_maps, across):
            for way in (0, 1):
                stage(k, way)

        @pl.when(k < fsdp - 1)
        def _():
            lax.fori_loop(0, 2, lambda way, none: finish(k, way), None)

        return carry

    lax.fori_loop(1, fsdp, pipeline, 0)

    core_u = remote(ubuf.at[t, :, p], ubuf.at[t, :, p], cu_s, cu_r, pair=1 - p)
    core_u.start()
    core_u.wait_send()
    remote(ubuf.at[t, :, 1 - p], ubuf.at[t, :, 1 - p], cu_s, cu_r, pair=1 - p).wait_recv()

    def x_u(i):
        return remote(
            ubuf.at[t], ubuf.at[t], xu_s.at[i], xu_r.at[t], tenant=lax.rem(t + i, tenant)
        )

    for i in range(1, tenant):
        x_u(i).start()
    lax.fori_loop(0, 2, lambda way, none: finish(fsdp - 1, way), None)

    sends = [
        remote(acc.at[1], pacc, part_s.at[0], part_r.at[0], pair=1 - p),
        remote(lacc.at[1], placc, part_s.at[1], part_r.at[1], pair=1 - p),
    ]
    for copy in sends:
        copy.start()
    for i in range(1, tenant):
        other = lax.rem(t + i, tenant)
        remote(ubuf.at[other], ubuf.at[other], xu_s.at[i], xu_r.at[other], tenant=other).wait_recv()
    for copy in sends:
        copy.wait_recv()

    outs = acc.shape[2]

    def up_map(m):
        return ubuf[m].reshape(outs, lanes)

    def choice(where):
        span = where.shape[1]
        row = lax.broadcasted_iota(jnp.int32, (lanes, span), 0)
        col = lax.broadcasted_iota(jnp.int32, (lanes, span), 1)
        mark = jnp.where(row < rank, where[0:1], where[1:2])
        return jnp.where((row & (rank - 1)) == (col & (rank - 1)), mark, 0.0)

    mine = choice(marks[...]).astype(BF16)
    sign = 1.0 - 2.0 * p.astype(F32)
    position = lax.broadcasted_iota(jnp.int32, (block, 1), 0).astype(F32)
    lane = lax.broadcasted_iota(jnp.int32, (block, lanes), 1)
    score[...] = jnp.zeros_like(score)
    weights = readout[...]

    for j in range(slots):
        rows = pl.ds(j * block, block)
        low = ((lacc[0, rows] + placc[rows]) * marks[j : j + 1]).astype(BF16)
        lowm[rows] = low
        mixed = acc[0, rows] + pacc[rows]
        for m in range(tenant):
            mixed += dot(low[:, m * lanes : (m + 1) * lanes], up_map(m), NT)
        acc[0, rows] = mixed
        gate = jax.nn.sigmoid(mixed)
        each = jnp.sum(weights * (mixed * gate), axis=1, keepdims=True)
        valid = (position < lengths[0, j].astype(F32)).astype(F32)
        total = jnp.sum(each * valid, axis=0, keepdims=True)
        score[j : j + 1] = jnp.broadcast_to(total, (1, score.shape[1]))
    swap = remote(score, pscore, score_s, score_r, pair=1 - p)
    swap.start()
    swap.wait_recv()

    rising = jnp.zeros((lanes, outs), F32)
    for j in range(slots):
        rows = pl.ds(j * block, block)
        logit = BETA * (sign * (score[j : j + 1] - pscore[j : j + 1]) - margins[j])
        alive = jnp.where(live[0] > j, 1.0, 0.0)
        down_side = -logit
        plus = jnp.maximum(down_side, 0.0) + jnp.log1p(jnp.exp(-jnp.abs(down_side)))
        loss_out[j] = (alive * plus)[0, 0]
        factor = (-BETA * alive * sign) * jax.nn.sigmoid(down_side)
        valid = (position < lengths[0, j].astype(F32)).astype(F32)
        mixed = acc[0, rows]
        gate = jax.nn.sigmoid(mixed)
        slope = gate * (1.0 + mixed * (1.0 - gate))
        turn = ((factor[:, :1] * valid) * weights * slope).astype(BF16)
        cot[rows] = turn
        small = jnp.zeros((block, lanes), F32)
        kept = jnp.zeros((block, lanes), F32)
        for m in range(tenant):
            span = slice(m * lanes, (m + 1) * lanes)
            grad = (dot(turn, up_map(m)) * marks[j : j + 1, span]).astype(BF16)
            small += dot(grad, mine[:, span], NT)
            kept += dot(lowm[rows, span], mine[:, span], NT)
        inside = (lane >= j * rank) & (lane < (j + 1) * rank)
        small = jnp.where(inside, small, 0.0)
        kept = jnp.where(inside, kept, 0.0)
        lgt[0, :, rows] = small.T.astype(BF16)
        rising += dot(kept.T.astype(BF16), turn)
    upsum[...] = rising.T.reshape(upsum.shape)
    mids = [
        remote(lgt.at[0], lgt.at[1], mid_s.at[0], mid_r.at[0], pair=1 - p),
        remote(upsum.at[:, 1 - p], upeer, mid_s.at[1], mid_r.at[1], pair=1 - p),
    ]
    for copy in mids:
        copy.start()

    part = ps.shape[3]

    def z_p(i, c):
        other = lax.rem(f + i, fsdp)
        return remote(ps.at[c, other], pr.at[c, f], p_s.at[c, i], p_r.at[c, f], fsdp=other)

    def z_p_in(i, c):
        other = lax.rem(f + i, fsdp)
        return remote(
            ps.at[c, other], pr.at[c, other], p_s.at[c, i], p_r.at[c, other], fsdp=other
        )

    def z_q(i):
        other = lax.rem(f + i, fsdp)
        return remote(uz.at[other], ur.at[f], q_s.at[i], q_r.at[f], fsdp=other)

    mids[0].wait_recv()

    def share(s, c):
        at = pl.ds(c * part, part)
        return (dot(lgt[0], tokens[0, s, :, at]) + dot(lgt[1], tokens[1, s, :, at])).astype(BF16)

    def send_share(c):
        def one(i, carry):
            s = lax.rem(f + i, fsdp)
            ps[c, s] = share(s, c)
            z_p(i, c).start()
            return carry

        lax.fori_loop(1, fsdp, one, 0)

    send_share(0)
    mids[1].wait_recv()
    for s in range(fsdp):
        uz[s] = (upsum[s, p] + upeer[s]).astype(BF16)
    for i in range(1, fsdp):
        z_q(i).start()
    for c in range(1, chunks):
        send_share(c)
    for c in range(chunks):
        pr[c, f] = share(f, c)
    ur[f] = uz[f]
    for i in range(1, fsdp):
        z_mark_in(i).wait_recv()

    def pick(m, s):
        at = pl.ds(pl.multiple_of(m * lanes, lanes), lanes)
        return choice(mbuf[s, :, at])

    def gathered(m, c):
        def add(s, big):
            return big + dot(pick(m, s).T.astype(BF16), pr[c, s])

        return lax.fori_loop(0, fsdp, add, jnp.zeros((lanes, part), F32))

    def gathered_up(m):
        def add(s, little):
            return little + dot(ur[s], pick(m, s).astype(BF16))

        return lax.fori_loop(0, fsdp, add, jnp.zeros((ur.shape[1], lanes), F32))

    outward = {}

    def send_down(c):
        for i in range(1, fsdp):
            z_p_in(i, c).wait_recv()
        for i in range(1, tenant):
            other = lax.rem(t + i, tenant)
            xs[c, i] = gathered(other, c).astype(BF16)
            copy = remote(xs.at[c, i], xr.at[c, i], xg_s.at[c, i], xg_r.at[c, i], tenant=other)
            copy.start()
            outward[c, i] = copy

    send_down(0)
    for i in range(1, fsdp):
        other = lax.rem(f + i, fsdp)
        remote(uz.at[other], ur.at[other], q_s.at[i], q_r.at[other], fsdp=other).wait_recv()
    for i in range(1, tenant):
        other = lax.rem(t + i, tenant)
        xus[i] = gathered_up(other).astype(BF16)
        copy = remote(xus.at[i], xur.at[i], xg_s.at[chunks, i], xg_r.at[chunks, i], tenant=other)
        copy.start()
        outward[chunks, i] = copy
    little = gathered_up(t)
    for c in range(1, chunks):
        send_down(c)
    for c in range(chunks):
        big = gathered(t, c)
        for i in range(1, tenant):
            outward[c, i].wait_recv()
            big += xr[c, i].astype(F32)
        down_out[:, pl.ds(c * part, part)] = big.astype(BF16)
    for i in range(1, tenant):
        outward[chunks, i].wait_recv()
        little += xur[i].astype(F32)
    for a in range(up_out.shape[0]):
        up_out[a] = little[:, a * rank : (a + 1) * rank].astype(BF16)
    for copy in outward.values():
        copy.wait_send()

    for way in (0, 1):

        @pl.when((f < fsdp - 1) if way == 0 else (f > 0))
        def _():
            z_w(f, way, base.at[quarter]).wait_send()
            z_d(f, way, down).wait_send()
            z_u(f, way, ubuf.at[t, f, p]).wait_send()

    for i in range(1, tenant):
        x_d(f, i, down).wait_send()
        x_u(i).wait_send()
    core_tokens(f).wait_send()

    def left(i, carry):
        core_tokens(lax.rem(f + i, fsdp)).wait_send()
        z_mark(i).wait_send()
        for c in range(chunks):
            z_p(i, c).wait_send()
        z_q(i).wait_send()
        return carry

    lax.fori_loop(1, fsdp, left, 0)

    def passed(n, carry):
        way = lax.rem(n, 2)
        s, fine, onward = place(n // 2 + 1, way)

        @pl.when(onward)
        def _():
            z_w(s, way, wbuf.at[s, quarter]).wait_send()
            z_d(s, way, dbuf.at[t, s]).wait_send()
            z_u(s, way, ubuf.at[t, s, p]).wait_send()

        @pl.when(fine)
        def _():
            if shares > 1:
                x_w(s).wait_send()
            for i in range(1, groups):
                for which in range(shares):
                    y_w(s, i, which).wait_send()
            for i in range(1, tenant):
                x_d(s, i, dbuf.at[t, s]).wait_send()

        return carry

    lax.fori_loop(0, 2 * (fsdp - 1), passed, 0)
    for copy in sends + [swap] + mids:
        copy.wait_send()


def shards(
    hidden,
    pair_adapter_index,
    live_block_count,
    lengths,
    adapter_storage_row,
    frozen_base_weight,
    adapter_down_maps,
    adapter_up_maps,
    readout,
    reference_score_margin,
):
    groups, fsdp = lax.axis_size("groups"), lax.axis_size("fsdp")
    tenant, pair = lax.axis_size("tenant"), lax.axis_size("pair")
    shares = 2 if tenant % 2 == 0 else 1
    _, slots, block, feature = hidden.shape
    held, width, rank = adapter_down_maps.shape
    outs = frozen_base_weight.shape[1]
    up_rows = adapter_up_maps.shape[1]
    lanes = slots * rank
    assert held == slots and pair == 2 and slots == 2
    parts = groups * shares
    count = slots * block

    base = frozen_base_weight.reshape(parts, width // parts, outs)
    down = adapter_down_maps.transpose(0, 2, 1).reshape(lanes, width)
    flat = hidden.reshape(count, feature)

    def kernel(*refs):
        view = BlockView(refs[7], width)
        step_kernel((groups, fsdp, tenant, shares, rank), *refs[:7], view, *refs[8:])

    any_space = pl.BlockSpec(memory_space=pl.ANY)
    vmem = pl.BlockSpec(memory_space=pltpu.VMEM)
    smem = pl.BlockSpec(memory_space=pltpu.SMEM)
    span = tenant * lanes
    chunks = 2
    dma = pltpu.SemaphoreType.DMA
    loss, down_grad, up_grad = pl.pallas_call(
        kernel,
        out_shape=(
            jax.ShapeDtypeStruct((slots,), F32),
            jax.ShapeDtypeStruct((lanes, width), BF16),
            jax.ShapeDtypeStruct(adapter_up_maps.shape, BF16),
        ),
        in_specs=[any_space] * 10,
        out_specs=(smem, vmem, vmem),
        scratch_shapes=[
            pltpu.SMEM(pair_adapter_index.shape, jnp.int32),
            pltpu.SMEM(live_block_count.shape, jnp.int32),
            pltpu.SMEM(lengths.shape, jnp.int32),
            pltpu.SMEM(adapter_storage_row.shape, jnp.int32),
            pltpu.SMEM(reference_score_margin.shape, F32),
            pltpu.VMEM((1, outs), F32),
            pltpu.VMEM(adapter_up_maps.shape, BF16),
            dma((7,)),
            pltpu.VMEM((8, span), F32),
            pltpu.VMEM((2, fsdp, count, width), BF16),
            pltpu.VMEM((fsdp, parts, width // parts, outs), BF16),
            pltpu.VMEM((tenant, fsdp, lanes, width), BF16),
            pltpu.VMEM((tenant, fsdp, 2, up_rows, lanes), BF16),
            pltpu.VMEM((fsdp, 8, span), F32),
            pltpu.VMEM((2, count, outs), F32),
            pltpu.VMEM((2, count, span), F32),
            pltpu.VMEM((count, outs), F32),
            pltpu.VMEM((count, span), F32),
            pltpu.VMEM((8, 128), F32),
            pltpu.VMEM((8, 128), F32),
            pltpu.VMEM((count, span), BF16),
            pltpu.VMEM((count, outs), BF16),
            pltpu.VMEM((2, lanes, count), BF16),
            pltpu.VMEM((fsdp, 2, up_rows, lanes), F32),
            pltpu.VMEM((fsdp, up_rows, lanes), F32),
            pltpu.VMEM((fsdp, up_rows, lanes), BF16),
            pltpu.VMEM((fsdp, up_rows, lanes), BF16),
            pltpu.VMEM((chunks, fsdp, lanes, width // chunks), BF16),
            pltpu.VMEM((chunks, fsdp, lanes, width // chunks), BF16),
            pltpu.VMEM((chunks, tenant, lanes, width // chunks), BF16),
            pltpu.VMEM((chunks, tenant, lanes, width // chunks), BF16),
            pltpu.VMEM((tenant, up_rows, lanes), BF16),
            pltpu.VMEM((tenant, up_rows, lanes), BF16),
            dma((fsdp,)), dma((2,)), dma((fsdp,)), dma((fsdp,)),
            dma((fsdp, 2)), dma((fsdp,)), dma((fsdp, 2)), dma((fsdp,)),
            dma((fsdp, 2)), dma((fsdp,)), dma((fsdp,)), dma((fsdp,)),
            dma((fsdp,)), dma((fsdp,)), dma((fsdp, tenant)), dma((tenant, fsdp)),
            dma((fsdp, groups, shares)), dma((fsdp, parts)),
            dma(()), dma(()), dma((tenant,)), dma((tenant,)),
            dma((2,)), dma((2,)), dma(()), dma(()), dma((2,)), dma((2,)),
            dma((chunks, fsdp)), dma((chunks, fsdp)), dma((fsdp,)), dma((fsdp,)),
            dma((chunks + 1, tenant)), dma((chunks + 1, tenant)),
        ],
        compiler_params=pltpu.CompilerParams(
            collective_id=0, has_side_effects=True, vmem_limit_bytes=61 * 1024 * 1024
        ),
        cost_estimate=pl.CostEstimate(
            flops=4 * count * feature * (outs + 2 * span), bytes_accessed=8 << 20, transcendentals=0
        ),
    )(
        pair_adapter_index, live_block_count, lengths, adapter_storage_row,
        reference_score_margin, readout.reshape(1, outs), adapter_up_maps, flat, base, down,
    )
    down_gradient = down_grad.reshape(held, rank, width).transpose(0, 2, 1)
    return loss, down_gradient, up_grad


class BlockView:
    def __init__(self, ref, width):
        self.ref, self.width = ref, width
        self.at = self

    def __getitem__(self, where):
        s, p = where
        start = pl.multiple_of((s * 2 + p) * self.width, self.width)
        return self.ref.at[:, pl.ds(start, self.width)]


def solution(mesh):
    return jax.shard_map(
        shards,
        mesh=mesh,
        in_specs=(
            P("pair", ("groups", "fsdp", "tenant"), None, None),
            P(("groups", "fsdp", "tenant")),
            P(("groups", "fsdp", "tenant")),
            P("pair", ("groups", "fsdp", "tenant")),
            P(),
            P(("fsdp", "pair"), None),
            P("tenant", ("fsdp", "pair"), None),
            P("tenant", ("fsdp", "pair"), None),
            P(),
            P(("groups", "fsdp", "tenant")),
        ),
        out_specs=(
            P(("groups", "fsdp", "tenant")),
            P(("groups", "tenant"), ("fsdp", "pair"), None),
            P(("groups", "tenant"), ("fsdp", "pair"), None),
        ),
        check_vma=False,
    )
```
